256 devices in a mesh: row: 32 (over z, x_lo, core), col: 8 (over x_hi, y).
Axes of the slice: x: 4 (x_hi: 2, x_lo: 2; x = x_hi * 2 + x_lo), y: 4, z: 8, core: 2. Of those that a mesh axis runs over, the one named last changes fastest.
Arguments:
- features: bfloat16 [65536, 128], P(('row', 'col')), may hold values from -6 to 6
- tiles: bfloat16 [32, 8, 96, 128, 128], P('row', 'col'), may hold values from -0.09375 to 0.09375
- tile_src: int32 [32, 8, 96], P('row', 'col'), may hold values from 0 to 15
- tile_dst: int32 [32, 8, 96], P('row', 'col'), may hold values from 0 to 63
- tile_count: int32 [32, 8], P('row', 'col'), may hold values from 12 to 96, as said below
- degree: int32 [65536], P(('row', 'col')), may hold values from 1 to 8
- w_self: bfloat16 [128, 128], replicated, may hold values from -0.5 to 0.5
- w_neigh: bfloat16 [128, 128], replicated, may hold values from -0.5 to 0.5
- bias: float32 [128], replicated, may hold values from -3 to 3
- upstream: bfloat16 [65536, 128], P(('row', 'col')), may hold values from -6 to 6
Outputs:
- hidden: bfloat16 [65536, 128], P(('row', 'col'))
- grad_features: bfloat16 [65536, 128], P(('row', 'col'))
- grad_self: float32 [128, 128], replicated
- grad_neigh: float32 [128, 128], replicated
- grad_bias: float32 [128], replicated
The draws below stay inside these ranges and needn't reach their ends.
Inputs may be any that keep to these rules, and one draw needn't show every extreme that they name: Slots at or past tile_count hold no edges; some device has all 96 slots live in every draw.
All inputs are finite; a program needn't handle non-finite values.
Results may differ from the reference program's by a relative error of at most 0.039.
The reference program's roundings to bfloat16 on the way (of `agg`, `dpre` and `scaled`) count: a program that leaves them out, or rounds other values in their place, can miss the bound.
Values may be sent and summed in bfloat16 or wider, within the bound.
No kernel may reach another device: no remote copies, remote signals or barrier semaphores. Data moves between devices by JAX's collectives and lax.ppermute only.
A program may use at most 64 MiB of HBM per device.

```python
import jax
import jax.numpy as jnp
from jax import lax

F = 128
H = 128
TILE = 128
NODE_DEV = 256
TILES_DEV = 96
NODES = 65536
SRC_NODES = 2048
DST_NODES = 8192
N_ROW = 32
N_COL = 8


def draw_tile_count(key, part):
    key = jax.random.fold_in(key, 7)
    first, second = jax.random.split(key)
    spread = jax.random.randint(first, (N_ROW, N_COL), 0, 64)
    least = TILES_DEV // 8
    counts = least + (TILES_DEV - least) * spread * spread // (63 * 63)
    where_full = jax.random.randint(second, (), 0, N_ROW * N_COL)
    counts = counts.reshape(-1).at[where_full].set(TILES_DEV)
    return counts.reshape(N_ROW, N_COL).astype(jnp.int32)


def set_ends(result, stream_key, low, high):
    spot = [jax.random.randint(jax.random.fold_in(stream_key, axis), (), 0, length) for axis, length in enumerate(result.shape)]
    widest = result.shape.index(max(result.shape))
    next_to = spot[:widest] + [(spot[widest] + 1) % result.shape[widest]] + spot[widest + 1:]
    return result.at[tuple(spot)].set(low).at[tuple(next_to)].set(high)


def levels(own_key, extent, cuts, low, top_value):
    def one(position, blocks):
        steps = jax.random.uniform(jax.random.fold_in(jax.random.fold_in(own_key, 6), position), (blocks,), jnp.float32, low / len(cuts), top_value / len(cuts))
        return jnp.repeat(jnp.exp(steps), extent[position] // blocks).reshape((-1,) + (1,) * (len(extent) - position - 1))

    gain = one(*cuts[0])
    for cut in cuts[1:]:
        gain = gain * one(*cut)
    return gain


def normal_values(stream_key, shape, scale, reach, cuts=(), held_as=jnp.bfloat16):
    entries = jax.random.normal(stream_key, shape, jnp.float32) * scale
    if len(cuts) > 0:
        entries = levels(stream_key, shape, cuts, -0.22, 0.18) * entries
    return jnp.clip(entries, min=-reach, max=reach).astype(held_as)


def setup_inputs(seed: int = 0) -> dict:
    arg_keys = jax.random.split(jax.random.key(seed), 11)
    return {
        "features": normal_values(arg_keys[0], (NODES, F), 1.0, 6.0, ((0, 256),)),
        "tiles": normal_values(arg_keys[1], (N_ROW, N_COL, TILES_DEV, TILE, TILE), (TILES_DEV * 48) ** -0.5, 0.09375, ((0, 32), (1, 8))),
        "tile_src": set_ends(jax.random.randint(arg_keys[2], (N_ROW, N_COL, TILES_DEV), 0, SRC_NODES // TILE), jax.random.fold_in(arg_keys[2], 1), 0, (SRC_NODES // TILE) - 1).astype(jnp.int32),
        "tile_dst": set_ends(jax.random.randint(arg_keys[3], (N_ROW, N_COL, TILES_DEV), 0, DST_NODES // TILE), jax.random.fold_in(arg_keys[3], 1), 0, (DST_NODES // TILE) - 1).astype(jnp.int32),
        "tile_count": draw_tile_count(jax.random.fold_in(arg_keys[10], 71), 0),
        "degree": set_ends(jax.random.randint(arg_keys[5], (NODES,), 1, 9), jax.random.fold_in(arg_keys[5], 1), 1, 8).astype(jnp.int32),
        "w_self": normal_values(arg_keys[6], (F, H), F ** -0.5, 0.5),
        "w_neigh": normal_values(arg_keys[7], (F, H), F ** -0.5, 0.5),
        "bias": normal_values(arg_keys[8], (H,), 0.5, 3.0, (), jnp.float32),
        "upstream": normal_values(arg_keys[9], (NODES, H), 1.0, 6.0, ((0, 256),)),
    }


def aggregate(field, tiles, tile_src, tile_dst, tile_count):
    fdim = field.shape[-1]
    grid = field.reshape(N_ROW, N_COL, NODE_DEV, fdim)
    nsrc = N_COL * NODE_DEV // TILE
    ndst = N_ROW * NODE_DEV // TILE
    slots = jnp.arange(TILES_DEV, dtype=jnp.int32)

    def one(total, index):
        rowi = index // N_COL
        coli = index % N_COL
        held = tiles[rowi, coli].astype(jnp.float32)
        live = slots < tile_count[rowi, coli]
        src_ids = tile_src[rowi, coli]
        dst_ids = tile_dst[rowi, coli]
        sources = lax.dynamic_index_in_dim(grid, rowi, 0, keepdims=False).reshape(nsrc, TILE, fdim)
        targets = lax.dynamic_index_in_dim(grid, coli, 1, keepdims=False).reshape(ndst, TILE, fdim)
        ahead = jnp.einsum('tab,tbf->taf', held, sources[src_ids].astype(jnp.float32))
        dst_part = jax.ops.segment_sum(ahead, jnp.where(live, dst_ids, ndst), ndst + 1)[:ndst]
        behind = jnp.einsum('tab,taf->tbf', held, targets[dst_ids].astype(jnp.float32))
        src_part = jax.ops.segment_sum(behind, jnp.where(live, src_ids, nsrc), nsrc + 1)[:nsrc]
        total = total.at[:, coli].add(dst_part.reshape(N_ROW, NODE_DEV, fdim))
        total = total.at[rowi].add(src_part.reshape(N_COL, NODE_DEV, fdim))
        return total, None

    start = jnp.zeros((N_ROW, N_COL, NODE_DEV, fdim), jnp.float32)
    total, _ = lax.scan(one, start, jnp.arange(N_ROW * N_COL, dtype=jnp.int32))
    return total.reshape(N_ROW * N_COL * NODE_DEV, fdim)


def reference(features, tiles, tile_src, tile_dst, tile_count, degree, w_self, w_neigh, bias, upstream):
    inverse = 1.0 / degree.astype(jnp.float32)
    summed = aggregate(features, tiles, tile_src, tile_dst, tile_count)
    agg = (summed * inverse[:, None]).astype(jnp.bfloat16)
    pre = jnp.dot(features, w_self, preferred_element_type=jnp.float32) + jnp.dot(agg, w_neigh, preferred_element_type=jnp.float32) + bias
    hidden = jnp.maximum(pre, 0.0).astype(jnp.bfloat16)
    dpre = jnp.where(pre > 0, upstream.astype(jnp.float32), jnp.zeros_like(pre)).astype(jnp.bfloat16)
    grad_self = jnp.dot(features.T, dpre, preferred_element_type=jnp.float32)
    grad_neigh = jnp.dot(agg.T, dpre, preferred_element_type=jnp.float32)
    grad_bias = jnp.sum(dpre.astype(jnp.float32), axis=0)
    scaled = (jnp.dot(dpre, w_neigh.T, preferred_element_type=jnp.float32) * inverse[:, None]).astype(jnp.bfloat16)
    carried = aggregate(scaled, tiles, tile_src, tile_dst, tile_count)
    grad_features = (jnp.dot(dpre, w_self.T, preferred_element_type=jnp.float32) + carried).astype(jnp.bfloat16)
    return hidden, grad_features, grad_self, grad_neigh, grad_bias
```

```python
import functools

import jax
import jax.numpy as jnp
from jax import lax
from jax.experimental import pallas as pl
from jax.experimental.pallas import tpu as pltpu
from jax.sharding import Mesh
from jax.sharding import PartitionSpec as P

TILE = 128
GROUP = 16
UNROLL = 8
ROW = ("z", "xl", "co")
COL = ("xh", "y")
SWAP = ((0, 1), (1, 0))
VMEM_LIMIT = 48 * 1024 * 1024


def whole(shape):
    return pl.BlockSpec(shape, lambda *_: (0,) * len(shape))


def steps(count, i):
    live = jnp.clip(count - i * GROUP, 0, GROUP)
    return (live + UNROLL - 1) // UNROLL


def ahead_kernel(src_ref, slot_ref, count_ref, field_ref, tiles_ref, keep_ref, send_ref, acc_ref):
    i = pl.program_id(0)
    half = keep_ref.shape[0]

    @pl.when(i == 0)
    def _():
        acc_ref[...] = jnp.zeros_like(acc_ref)

    def step(k, carry):
        outs = []
        for u in range(UNROLL):
            j = k * UNROLL + u
            t = i * GROUP + j
            outs.append(
                jnp.dot(
                    tiles_ref[j],
                    field_ref[jnp.minimum(src_ref[t], 15)],
                    preferred_element_type=jnp.float32,
                )
            )
        for u in range(UNROLL):
            t = i * GROUP + k * UNROLL + u
            acc_ref[slot_ref[t]] += outs[u]
        return carry

    lax.fori_loop(0, steps(count_ref[0], i), step, 0)

    @pl.when(i == pl.num_programs(0) - 1)
    def _():
        keep_ref[...] = acc_ref[:half]
        send_ref[...] = acc_ref[half : 2 * half].astype(send_ref.dtype)


def ahead(field, tiles, src, slot, count):
    n = tiles.shape[0]
    half = 32
    return pl.pallas_call(
        ahead_kernel,
        grid_spec=pltpu.PrefetchScalarGridSpec(
            num_scalar_prefetch=3,
            grid=(n // GROUP,),
            in_specs=[whole(field.shape), pl.BlockSpec((GROUP, TILE, TILE), lambda i, *_: (i, 0, 0))],
            out_specs=[whole((half, TILE, TILE))] * 2,
            scratch_shapes=[pltpu.VMEM((2 * half + 1, TILE, TILE), jnp.float32)],
        ),
        out_shape=[
            jax.ShapeDtypeStruct((half, TILE, TILE), jnp.float32),
            jax.ShapeDtypeStruct((half, TILE, TILE), jnp.bfloat16),
        ],
        compiler_params=pltpu.CompilerParams(vmem_limit_bytes=VMEM_LIMIT),
        cost_estimate=pl.CostEstimate(flops=2 * n * TILE**3, bytes_accessed=n * TILE * TILE * 2, transcendentals=0),
    )(src, slot, count, field, tiles)


def behind_kernel(src_ref, slot_ref, count_ref, g0, g1, g2, g3, tiles_ref, out_ref, field_ref, acc_ref):
    i = pl.program_id(0)
    n = g0.shape[0]

    @pl.when(i == 0)
    def _():
        acc_ref[...] = jnp.zeros_like(acc_ref)
        for k, g in enumerate((g0, g1, g2, g3)):
            field_ref[k * n : (k + 1) * n] = g[...]
        field_ref[4 * n] = jnp.zeros_like(field_ref[4 * n])

    def step(k, carry):
        outs = []
        for u in range(UNROLL):
            j = k * UNROLL + u
            t = i * GROUP + j
            outs.append(
                jnp.dot(field_ref[slot_ref[t]], tiles_ref[j], preferred_element_type=jnp.float32)
            )
        for u in range(UNROLL):
            t = i * GROUP + k * UNROLL + u
            acc_ref[src_ref[t]] += outs[u]
        return carry

    lax.fori_loop(0, steps(count_ref[0], i), step, 0)

    @pl.when(i == pl.num_programs(0) - 1)
    def _():
        for k in range(out_ref.shape[0]):
            out_ref[k] = acc_ref[k].T.astype(out_ref.dtype)


def behind(parts, tiles, src, slot, count):
    n = tiles.shape[0]
    nsrc = 16
    return pl.pallas_call(
        behind_kernel,
        grid_spec=pltpu.PrefetchScalarGridSpec(
            num_scalar_prefetch=3,
            grid=(n // GROUP,),
            in_specs=[whole(p.shape) for p in parts]
            + [pl.BlockSpec((GROUP, TILE, TILE), lambda i, *_: (i, 0, 0))],
            out_specs=whole((nsrc, TILE, TILE)),
            scratch_shapes=[
                pltpu.VMEM((65, TILE, TILE), jnp.bfloat16),
                pltpu.VMEM((nsrc + 1, TILE, TILE), jnp.float32),
            ],
        ),
        out_shape=jax.ShapeDtypeStruct((nsrc, TILE, TILE), jnp.bfloat16),
        compiler_params=pltpu.CompilerParams(vmem_limit_bytes=VMEM_LIMIT),
        cost_estimate=pl.CostEstimate(flops=2 * n * TILE**3, bytes_accessed=n * TILE * TILE * 2, transcendentals=0),
    )(src, slot, count, *parts, tiles)


def swap(x, axis):
    return lax.ppermute(x, axis, SWAP)


def spread(x, axes, n):
    return lax.all_to_all(jnp.broadcast_to(x[None], (n,) + x.shape), axes, 0, 0, tiled=True)


def turned(x):
    return x.reshape(-1, TILE, TILE).swapaxes(1, 2)


def aggregate(field, field_t, tiles, src, slot, count):
    with jax.named_scope("gather_col"):
        sources = spread(field.reshape(-1, TILE, TILE), COL, 8).reshape(-1, TILE, TILE)
    with jax.named_scope("gather_row"):
        g00 = spread(field_t, "z", 8).reshape(-1, TILE, TILE)
        g01 = swap(g00, "xl")
        g10 = swap(g00, "co")
        g11 = swap(g01, "co")
    with jax.named_scope("ahead"):
        keep, send = ahead(sources, tiles, src, slot, count)
    with jax.named_scope("behind"):
        back = behind((g00, g01, g10, g11), tiles, src, slot, count)
    with jax.named_scope("scatter_row"):
        got = swap(send, "co")
        both = keep + got.astype(jnp.float32)
        got = swap(both[16:].astype(jnp.bfloat16), "xl")
        four = both[:16] + got.astype(jnp.float32)
        first = lax.all_to_all(
            four.astype(jnp.bfloat16).reshape(8, -1, TILE), "z", 0, 0, tiled=True
        )
    with jax.named_scope("scatter_col"):
        second = lax.all_to_all(back.reshape(8, -1, TILE), COL, 0, 0, tiled=True)
    return first, second


def total(first, second):
    return jnp.sum(first.astype(jnp.float32), axis=0) + jnp.sum(second.astype(jnp.float32), axis=0)


def body(features, tiles, tile_src, tile_dst, tile_count, degree, w_self, w_neigh, bias, upstream):
    held = tiles[0, 0]
    count = tile_count[0]
    live = jnp.arange(held.shape[0], dtype=jnp.int32) < count[0]
    src = jnp.where(live, tile_src[0, 0], 16)
    dst = tile_dst[0, 0]
    other_co = ((dst // 2) % 2) ^ lax.axis_index("co")
    other_xl = ((dst // 4) % 2) ^ lax.axis_index("xl")
    slot = (other_co * 2 + other_xl) * 16 + (dst // 8) * 2 + dst % 2
    slot = jnp.where(live, slot, 64)
    inverse = 1.0 / degree.astype(jnp.float32)

    first, second = aggregate(features, turned(features), held, src, slot, count)
    agg = (total(first, second) * inverse[:, None]).astype(jnp.bfloat16)
    pre = (
        jnp.dot(features, w_self, preferred_element_type=jnp.float32)
        + jnp.dot(agg, w_neigh, preferred_element_type=jnp.float32)
        + bias
    )
    hidden = jnp.maximum(pre, 0.0).astype(jnp.bfloat16)
    dpre = jnp.where(pre > 0, upstream.astype(jnp.float32), 0.0).astype(jnp.bfloat16)
    scaled = (
        jnp.dot(dpre, w_neigh.T, preferred_element_type=jnp.float32) * inverse[:, None]
    ).astype(jnp.bfloat16)
    with jax.named_scope("weights"):
        local = jnp.concatenate(
            [
                jnp.dot(features.T, dpre, preferred_element_type=jnp.float32),
                jnp.dot(agg.T, dpre, preferred_element_type=jnp.float32),
                jnp.broadcast_to(jnp.sum(dpre.astype(jnp.float32), axis=0)[None] / 8, (8, TILE)),
            ]
        )
        for axis, n in (("co", 2), ("xl", 2), ("z", 8), ("xh", 2), ("y", 4)):
            d = 1
            while d < n:
                local = local + lax.ppermute(local, axis, [(i, i ^ d) for i in range(n)])
                d *= 2
    first, second = aggregate(scaled, turned(scaled), held, src, slot, count)
    carried = total(first, second)
    grad_features = (jnp.dot(dpre, w_self.T, preferred_element_type=jnp.float32) + carried).astype(
        jnp.bfloat16
    )
    return (
        hidden,
        grad_features,
        local[:TILE],
        local[TILE : 2 * TILE],
        jnp.sum(local[2 * TILE :], axis=0),
    )


def solution(mesh):
    fine = Mesh(mesh.devices.reshape(8, 2, 2, 2, 4), ROW + COL)
    nodes = P(ROW + COL, None)
    return jax.shard_map(
        body,
        mesh=fine,
        in_specs=(
            nodes,
            P(ROW, COL, None, None, None),
            P(ROW, COL, None),
            P(ROW, COL, None),
            P(ROW, COL),
            P(ROW + COL),
            P(),
            P(),
            P(),
            nodes,
        ),
        out_specs=(nodes, nodes, P(), P(), P()),
        check_vma=False,
    )
```

```python
import jax
import jax.numpy as jnp
from jax import lax
from jax.experimental import pallas as pl
from jax.experimental.pallas import tpu as pltpu
from jax.sharding import Mesh
from jax.sharding import PartitionSpec as P

TILE = 128
UNROLL = 8
GROUP = 16
ROW = ("z", "xl", "co")
COL = ("xh", "y")
HALF_SCALE = 2.0
VMEM_LIMIT = 16 * 1024 * 1024


def whole(shape):
    return pl.BlockSpec(shape, lambda *_: (0,) * len(shape))


def multiply(tiles_hbm, tiles_ref, sems, count_ref, acc_ref, ids_ref, prepare, product):
    count = count_ref[0]
    groups = tiles_ref.shape[0] // GROUP

    def chunk(i):
        part = pl.ds(i * GROUP, GROUP)
        return pltpu.make_async_copy(tiles_hbm.at[part], tiles_ref.at[part], sems.at[i])

    for i in range(groups):
        chunk(i).start()
    prepare()
    acc_ref[...] = jnp.zeros_like(acc_ref)

    def step(k, carry):
        base = k * UNROLL
        outs = [product(base + u) for u in range(UNROLL)]
        for u in range(UNROLL):
            acc_ref[ids_ref[base + u]] += outs[u]
        return carry

    last = (count + UNROLL - 1) // UNROLL
    per = GROUP // UNROLL
    for i in range(groups):
        chunk(i).wait()
        lax.fori_loop(jnp.minimum(i * per, last), jnp.minimum((i + 1) * per, last), step, 0)


def ahead_kernel(src_ref, slot_ref, count_ref, f0, f1, f2, f3, tiles_hbm,
                 keep_ref, send_ref, field_ref, acc_ref, tiles_ref, sems):
    def prepare():
        for k, f in enumerate((f0, f1, f2, f3)):
            for h in range(2):
                field_ref[k * 4 + h * 2 : k * 4 + h * 2 + 2] = f[h]
        field_ref[16] = jnp.zeros_like(field_ref[16])

    def product(t):
        return jnp.dot(tiles_ref[t], field_ref[src_ref[t]], preferred_element_type=jnp.float32)

    multiply(tiles_hbm, tiles_ref, sems, count_ref, acc_ref, slot_ref, prepare, product)
    send_ref[...] = acc_ref[32:64].astype(send_ref.dtype)
    keep_ref[...] = acc_ref[:32]


def behind_kernel(src_ref, slot_ref, count_ref, g0, g1, tiles_hbm,
                  keep_ref, s1, s2, s3, field_ref, acc_ref, tiles_ref, sems):
    n = g0.shape[0]

    def prepare():
        field_ref[:n] = g0[...]
        field_ref[n : 2 * n] = g1[...]
        field_ref[2 * n] = jnp.zeros_like(field_ref[2 * n])

    def product(t):
        return jnp.dot(field_ref[slot_ref[t]], tiles_ref[t], preferred_element_type=jnp.float32)

    multiply(tiles_hbm, tiles_ref, sems, count_ref, acc_ref, src_ref, prepare, product)
    for p, ref in enumerate((keep_ref, s1, s2, s3)):
        for k in range(4):
            ref[k] = acc_ref[p * 4 + k].T.astype(ref.dtype)


def products(kernel, parts, tiles, src, slot, count, nfield, nacc, outs, name):
    n = tiles.shape[0]
    return pl.pallas_call(
        kernel,
        in_specs=[pl.BlockSpec(memory_space=pltpu.SMEM)] * 3
        + [pl.BlockSpec(memory_space=pltpu.VMEM)] * len(parts)
        + [pl.BlockSpec(memory_space=pltpu.HBM)],
        out_specs=[pl.BlockSpec(memory_space=pltpu.VMEM) for _ in outs],
        out_shape=[jax.ShapeDtypeStruct((k, TILE, TILE), dtype) for k, dtype in outs],
        scratch_shapes=[
            pltpu.VMEM((nfield + 1, TILE, TILE), jnp.bfloat16),
            pltpu.VMEM((nacc + 1, TILE, TILE), jnp.float32),
            pltpu.VMEM((n, TILE, TILE), tiles.dtype),
            pltpu.SemaphoreType.DMA((n // GROUP,)),
        ],
        compiler_params=pltpu.CompilerParams(vmem_limit_bytes=VMEM_LIMIT),
        cost_estimate=pl.CostEstimate(
            flops=16 * n * TILE**3, bytes_accessed=n * TILE * TILE * 2, transcendentals=0
        ),
        name=name,
    )(src, slot, count, *parts, pltpu.with_memory_space_constraint(tiles, pltpu.HBM))


def flip(x, axis, d=1):
    n = lax.axis_size(axis)
    return lax.ppermute(x, axis, [(i, i ^ d) for i in range(n)])


def tie(*xs):
    return lax.optimization_barrier(xs)


def pack(x, exact):
    return (x * HALF_SCALE).astype(jnp.float16) if exact else x.astype(jnp.bfloat16)


def unpack(x):
    wide = x.astype(jnp.float32)
    return wide * (1.0 / HALF_SCALE) if x.dtype == jnp.float16 else wide


def aggregate(field, copies, tiles, src, slot, count, exact, side):
    with jax.named_scope("gather_row"):
        g0 = lax.all_to_all(copies, ("z", "xl"), 0, 0, tiled=True).reshape(-1, TILE, TILE)
    with jax.named_scope("gather_col"):
        (other,) = side(0, flip(field, "xh"))
        pair = jnp.stack([field, other])
        cols = side(1, pair, *(flip(pair, "y", k) for k in (1, 2, 3)))
    with jax.named_scope("ahead"):
        keep, send = products(
            ahead_kernel, cols, tiles, src, slot, count, 16, 64, ((32, jnp.float32), (32, jnp.bfloat16)), "ahead"
        )
        keep, send = side(2, keep, send)
    with jax.named_scope("scatter_row"):
        both = pack(keep + flip(send, "co").astype(jnp.float32), exact)
    g0, both = tie(*side(3, g0), both)
    with jax.named_scope("scatter_row"):
        first = lax.all_to_all(both.reshape(16, -1, TILE), ("z", "xl"), 0, 0, tiled=True)
    with jax.named_scope("gather_row"):
        (g1,) = side(4, flip(g0, "co"))
    with jax.named_scope("behind"):
        back, *sends = products(
            behind_kernel, (g0, g1), tiles, src, slot, count, 64, 16, ((4, jnp.float32),) + ((4, jnp.bfloat16),) * 3, "behind"
        )
        back, *sends = side(5, back, *sends)
    with jax.named_scope("scatter_col"):
        for k in (1, 2, 3):
            back = back + flip(sends[k - 1], "y", k).astype(jnp.float32)
        (back,) = side(6, back)
        last = flip(pack(back[2:], exact), "xh")
    (last,) = side(7, last)
    return first, back[:2].reshape(-1, TILE), last.reshape(-1, TILE)


def total(first, back, last):
    return jnp.sum(unpack(first), axis=0) + back + unpack(last)


def prepare_kernel(features_ref, copies_ref):
    for h in range(2):
        block = features_ref[h * TILE : (h + 1) * TILE].astype(jnp.float32).T.astype(jnp.bfloat16)
        for k in range(copies_ref.shape[0]):
            copies_ref[k, h] = block


def prepare(features):
    return pl.pallas_call(
        prepare_kernel,
        out_shape=jax.ShapeDtypeStruct((16, 2, TILE, TILE), jnp.bfloat16),
        compiler_params=pltpu.CompilerParams(vmem_limit_bytes=VMEM_LIMIT),
        name="prepare",
    )(features)


def middle_kernel(summed_ref, inverse_ref, features_ref, upstream_ref, w_self_ref, w_neigh_ref, bias_ref,
                  hidden_ref, scaled_ref, copies_ref, base_ref, local_ref):
    def dot(a, b, dims):
        return lax.dot_general(a, b, (dims, ((), ())), preferred_element_type=jnp.float32)

    features = features_ref[...]
    inverse = inverse_ref[...]
    w_self, w_neigh = w_self_ref[...], w_neigh_ref[...]
    agg = (summed_ref[...] * inverse).astype(jnp.bfloat16)
    pre = dot(features, w_self, ((1,), (0,))) + dot(agg, w_neigh, ((1,), (0,))) + bias_ref[...]
    hidden_ref[...] = jnp.maximum(pre, 0.0).astype(jnp.bfloat16)
    wide = jnp.where(pre > 0, upstream_ref[...].astype(jnp.float32), 0.0)
    dpre = wide.astype(jnp.bfloat16)
    scaled = (dot(dpre, w_neigh, ((1,), (1,))) * inverse).astype(jnp.bfloat16)
    scaled_ref[...] = scaled
    for h in range(2):
        block = scaled[h * TILE : (h + 1) * TILE].astype(jnp.float32).T.astype(jnp.bfloat16)
        for k in range(copies_ref.shape[0]):
            copies_ref[k, h] = block
    base_ref[...] = dot(dpre, w_self, ((1,), (1,)))
    local_ref[0, :TILE] = dot(features, dpre, ((0,), (0,)))
    local_ref[1, :TILE] = dot(agg, dpre, ((0,), (0,)))
    wide = wide.reshape(-1, 8, TILE)
    for h in range(2):
        local_ref[h, TILE:] = jnp.sum(wide, axis=0)


def middle(summed, inverse, features, upstream, w_self, w_neigh, bias):
    nodes = features.shape
    return pl.pallas_call(
        middle_kernel,
        out_shape=[
            jax.ShapeDtypeStruct(nodes, jnp.bfloat16),
            jax.ShapeDtypeStruct(nodes, jnp.bfloat16),
            jax.ShapeDtypeStruct((16, 2, TILE, TILE), jnp.bfloat16),
            jax.ShapeDtypeStruct(nodes, jnp.float32),
            jax.ShapeDtypeStruct((2, TILE + 8, TILE), jnp.float32),
        ],
        compiler_params=pltpu.CompilerParams(vmem_limit_bytes=VMEM_LIMIT),
        name="middle",
    )(summed, inverse, features, upstream, w_self, w_neigh, bias)


def final_kernel(co_ref, first_ref, back_ref, last_ref, base_ref, w_ref, grad_ref, self_ref, neigh_ref, bias_ref):
    carried = total(first_ref[...], back_ref[...], last_ref[...])
    grad_ref[...] = (base_ref[...] + carried).astype(grad_ref.dtype)
    co = co_ref[0]
    self_ref[...] = w_ref[co, :TILE]
    neigh_ref[...] = w_ref[1 - co, :TILE]
    bias_ref[...] = jnp.sum(w_ref[0, TILE:], axis=0, keepdims=True)


def final(co, first, back, last, base, weights):
    shapes = ((base.shape, jnp.bfloat16), ((TILE, TILE), jnp.float32), ((TILE, TILE), jnp.float32), ((1, TILE), jnp.float32))
    args = (first, back, last, base, weights)
    return pl.pallas_call(
        final_kernel,
        grid_spec=pltpu.PrefetchScalarGridSpec(
            num_scalar_prefetch=1,
            grid=(1,),
            in_specs=[whole(x.shape) for x in args],
            out_specs=[whole(x) for x, _ in shapes],
        ),
        out_shape=[jax.ShapeDtypeStruct(x, dtype) for x, dtype in shapes],
        compiler_params=pltpu.CompilerParams(vmem_limit_bytes=VMEM_LIMIT),
        name="final",
    )(co, *args)


STEPS = ((("co", 1),), (), (), (("z", 1, 2, 3),), (("xl", 1),), (("xh", 1),), (("y", 1, 2, 3),), (("z", 4),))


def body(features, tiles, tile_src, tile_dst, tile_count, degree, w_self, w_neigh, bias, upstream):
    held = tiles[0, 0]
    count = tile_count[0]
    co, xl, xh, y = (lax.axis_index(a) for a in ("co", "xl", "xh", "y"))
    live = jnp.arange(held.shape[0], dtype=jnp.int32) < count[0]
    src, dst = tile_src[0, 0], tile_dst[0, 0]
    src = ((((src // 2) % 4) ^ y) * 2 + ((src // 8) ^ xh)) * 2 + src % 2
    src = jnp.where(live, src, 16)
    other = ((dst // 2) % 2) ^ co
    slot = other * 32 + (dst // 4) * 2 + dst % 2
    slot = jnp.where(live, slot, 64)
    inverse = jnp.broadcast_to(1.0 / degree.astype(jnp.float32)[:, None], features.shape)

    blocks = features.reshape(-1, TILE, TILE)
    parts = aggregate(blocks, prepare(features), held, src, slot, count, True, lambda k, *xs: xs)
    hidden, scaled, copies, base, local = middle(
        total(*parts), inverse, features, upstream, w_self, w_neigh, bias.reshape(1, -1)
    )

    weights = [local]

    def side(k, *xs):
        with jax.named_scope("weights"):
            w = weights[0]
            if k == 0:
                mine = lax.dynamic_index_in_dim(w, co, 0, keepdims=False)
                w = mine + flip(lax.dynamic_index_in_dim(w, 1 - co, 0, keepdims=False), "co")
            else:
                for axis, *hops in STEPS[k]:
                    w = sum((flip(w, axis, d) for d in hops), w)
            *xs, weights[0] = tie(*xs, w)
        return xs

    parts = aggregate(scaled.reshape(-1, TILE, TILE), copies, held, src, slot, count, False, side)
    with jax.named_scope("weights"):
        pair = jnp.stack([weights[0], flip(weights[0], "co")])
    grad_features, grad_self, grad_neigh, grad_bias = final(co.reshape(1), *parts, base, pair)
    return hidden, grad_features, grad_self, grad_neigh, grad_bias[0]


def solution(mesh):
    fine = Mesh(mesh.devices.reshape(8, 2, 2, 2, 4), ROW + COL)
    nodes = P(ROW + COL, None)
    return jax.shard_map(
        body,
        mesh=fine,
        in_specs=(
            nodes,
            P(ROW, COL, None, None, None),
            P(ROW, COL, None),
            P(ROW, COL, None),
            P(ROW, COL),
            P(ROW + COL),
            P(),
            P(),
            P(),
            nodes,
        ),
        out_specs=(nodes, nodes, P(), P(), P()),
        check_vma=False,
    )
```

```python
import jax
import jax.numpy as jnp
from jax import lax
from jax.experimental import pallas as pl
from jax.experimental.pallas import tpu as pltpu
from jax.sharding import Mesh
from jax.sharding import PartitionSpec as P

TILE = 128
UNROLL = 8
GROUP = 16
ROW = ("z", "xl", "co")
COL = ("xh", "y")
HALF_SCALE = 2.0
VMEM_LIMIT = 16 * 1024 * 1024


def whole(shape):
    return pl.BlockSpec(shape, lambda *_: (0,) * len(shape))


def multiply(tiles_hbm, tiles_ref, sems, count_ref, acc_ref, ids_ref, prepare, product):
    count = count_ref[0]
    groups = tiles_ref.shape[0] // GROUP

    def chunk(i):
        part = pl.ds(i * GROUP, GROUP)
        return pltpu.make_async_copy(tiles_hbm.at[part], tiles_ref.at[part], sems.at[i])

    for i in range(groups):
        chunk(i).start()
    prepare()
    acc_ref[...] = jnp.zeros_like(acc_ref)

    def step(k, carry):
        base = k * UNROLL
        outs = [product(base + u) for u in range(UNROLL)]
        for u in range(UNROLL):
            acc_ref[ids_ref[base + u]] += outs[u]
        return carry

    last = (count + UNROLL - 1) // UNROLL
    per = GROUP // UNROLL
    for i in range(groups):
        chunk(i).wait()
        lax.fori_loop(jnp.minimum(i * per, last), jnp.minimum((i + 1) * per, last), step, 0)


def ahead_kernel(src_ref, slot_ref, count_ref, f0, f1, f2, f3, tiles_hbm,
                 keep_ref, send_ref, field_ref, acc_ref, tiles_ref, sems):
    def prepare():
        for k, f in enumerate((f0, f1, f2, f3)):
            for h in range(2):
                field_ref[k * 4 + h * 2 : k * 4 + h * 2 + 2] = f[h]
        field_ref[16] = jnp.zeros_like(field_ref[16])

    def product(t):
        return jnp.dot(tiles_ref[t], field_ref[src_ref[t]], preferred_element_type=jnp.float32)

    multiply(tiles_hbm, tiles_ref, sems, count_ref, acc_ref, slot_ref, prepare, product)
    send_ref[...] = acc_ref[32:64].astype(send_ref.dtype)
    keep_ref[...] = acc_ref[:32]


def behind_kernel(src_ref, slot_ref, count_ref, g0, g1, tiles_hbm,
                  keep_ref, s1, s2, s3, field_ref, acc_ref, tiles_ref, sems):
    n = g0.shape[0]

    def prepare():
        field_ref[:n] = g0[...]
        field_ref[n : 2 * n] = g1[...]
        field_ref[2 * n] = jnp.zeros_like(field_ref[2 * n])

    def product(t):
        return jnp.dot(field_ref[slot_ref[t]], tiles_ref[t], preferred_element_type=jnp.float32)

    multiply(tiles_hbm, tiles_ref, sems, count_ref, acc_ref, src_ref, prepare, product)
    for p, ref in enumerate((keep_ref, s1, s2, s3)):
        for k in range(4):
            ref[k] = acc_ref[p * 4 + k].T.astype(ref.dtype)


def products(kernel, parts, tiles, src, slot, count, nfield, nacc, outs, name):
    n = tiles.shape[0]
    return pl.pallas_call(
        kernel,
        in_specs=[pl.BlockSpec(memory_space=pltpu.SMEM)] * 3
        + [pl.BlockSpec(memory_space=pltpu.VMEM)] * len(parts)
        + [pl.BlockSpec(memory_space=pltpu.HBM)],
        out_specs=[pl.BlockSpec(memory_space=pltpu.VMEM) for _ in outs],
        out_shape=[jax.ShapeDtypeStruct((k, TILE, TILE), dtype) for k, dtype in outs],
        scratch_shapes=[
            pltpu.VMEM((nfield + 1, TILE, TILE), jnp.bfloat16),
            pltpu.VMEM((nacc + 1, TILE, TILE), jnp.float32),
            pltpu.VMEM((n, TILE, TILE), tiles.dtype),
            pltpu.SemaphoreType.DMA((n // GROUP,)),
        ],
        compiler_params=pltpu.CompilerParams(vmem_limit_bytes=VMEM_LIMIT),
        cost_estimate=pl.CostEstimate(
            flops=16 * n * TILE**3, bytes_accessed=n * TILE * TILE * 2, transcendentals=0
        ),
        name=name,
    )(src, slot, count, *parts, pltpu.with_memory_space_constraint(tiles, pltpu.HBM))


def flip(x, axis, d=1):
    n = lax.axis_size(axis)
    return lax.ppermute(x, axis, [(i, i ^ d) for i in range(n)])


def tie(*xs):
    return lax.optimization_barrier(xs)


def pack(x, exact):
    return (x.astype(jnp.float32) * HALF_SCALE).astype(jnp.float16) if exact else x.astype(jnp.bfloat16)


def unpack(x):
    wide = x.astype(jnp.float32)
    return wide * (1.0 / HALF_SCALE) if x.dtype == jnp.float16 else wide


def aggregate(field, copies, tiles, src, slot, count, exact, side):
    sent = jnp.float32 if exact else jnp.bfloat16
    with jax.named_scope("gather_row"):
        g0 = lax.all_to_all(copies, ("z", "xl"), 0, 0, tiled=True).reshape(-1, TILE, TILE)
    with jax.named_scope("gather_col"):
        (other,) = side(0, flip(field, "xh"))
        pair = jnp.stack([field, other])
        cols = side(1, pair, *(flip(pair, "y", k) for k in (1, 2, 3)))
    with jax.named_scope("ahead"):
        keep, send = products(
            ahead_kernel, cols, tiles, src, slot, count, 16, 64, ((32, jnp.float32), (32, sent)), "ahead"
        )
        keep, send = side(2, keep, send)
    with jax.named_scope("scatter_row"):
        both = pack(keep + unpack(flip(pack(send, exact), "co")), exact)
    g0, both = tie(*side(3, g0), both)
    with jax.named_scope("scatter_row"):
        first = lax.all_to_all(both.reshape(16, -1, TILE), ("z", "xl"), 0, 0, tiled=True)
    with jax.named_scope("gather_row"):
        (g1,) = side(4, flip(g0, "co"))
    with jax.named_scope("behind"):
        back, *sends = products(
            behind_kernel, (g0, g1), tiles, src, slot, count, 64, 16, ((4, jnp.float32),) + ((4, sent),) * 3, "behind"
        )
        back, *sends = side(5, back, *sends)
    with jax.named_scope("scatter_col"):
        for k in (1, 2, 3):
            back = back + unpack(flip(pack(sends[k - 1], exact), "y", k))
        (back,) = side(6, back)
        last = flip(pack(back[2:], exact), "xh")
    (last,) = side(7, last)
    return first, back[:2].reshape(-1, TILE), last.reshape(-1, TILE)


def total(first, back, last):
    return jnp.sum(unpack(first), axis=0) + back + unpack(last)


def prepare_kernel(features_ref, copies_ref):
    for h in range(2):
        block = features_ref[h * TILE : (h + 1) * TILE].astype(jnp.float32).T.astype(jnp.bfloat16)
        for k in range(copies_ref.shape[0]):
            copies_ref[k, h] = block


def prepare(features):
    return pl.pallas_call(
        prepare_kernel,
        out_shape=jax.ShapeDtypeStruct((16, 2, TILE, TILE), jnp.bfloat16),
        compiler_params=pltpu.CompilerParams(vmem_limit_bytes=VMEM_LIMIT),
        name="prepare",
    )(features)


def middle_kernel(summed_ref, inverse_ref, features_ref, upstream_ref, w_self_ref, w_neigh_ref, bias_ref,
                  hidden_ref, scaled_ref, copies_ref, base_ref, local_ref):
    def dot(a, b, dims):
        return lax.dot_general(a, b, (dims, ((), ())), preferred_element_type=jnp.float32)

    features = features_ref[...]
    inverse = inverse_ref[...]
    w_self, w_neigh = w_self_ref[...], w_neigh_ref[...]
    agg = (summed_ref[...] * inverse).astype(jnp.bfloat16)
    pre = dot(features, w_self, ((1,), (0,))) + dot(agg, w_neigh, ((1,), (0,))) + bias_ref[...]
    hidden_ref[...] = jnp.maximum(pre, 0.0).astype(jnp.bfloat16)
    wide = jnp.where(pre > 0, upstream_ref[...].astype(jnp.float32), 0.0)
    dpre = wide.astype(jnp.bfloat16)
    scaled = (dot(dpre, w_neigh, ((1,), (1,))) * inverse).astype(jnp.bfloat16)
    scaled_ref[...] = scaled
    for h in range(2):
        block = scaled[h * TILE : (h + 1) * TILE].astype(jnp.float32).T.astype(jnp.bfloat16)
        for k in range(copies_ref.shape[0]):
            copies_ref[k, h] = block
    base_ref[...] = dot(dpre, w_self, ((1,), (1,)))
    local_ref[0, :TILE] = dot(features, dpre, ((0,), (0,)))
    local_ref[1, :TILE] = dot(agg, dpre, ((0,), (0,)))
    wide = wide.reshape(-1, 8, TILE)
    for h in range(2):
        local_ref[h, TILE:] = jnp.sum(wide, axis=0)


def middle(summed, inverse, features, upstream, w_self, w_neigh, bias):
    nodes = features.shape
    return pl.pallas_call(
        middle_kernel,
        out_shape=[
            jax.ShapeDtypeStruct(nodes, jnp.bfloat16),
            jax.ShapeDtypeStruct(nodes, jnp.bfloat16),
            jax.ShapeDtypeStruct((16, 2, TILE, TILE), jnp.bfloat16),
            jax.ShapeDtypeStruct(nodes, jnp.float32),
            jax.ShapeDtypeStruct((2, TILE + 8, TILE), jnp.float32),
        ],
        compiler_params=pltpu.CompilerParams(vmem_limit_bytes=VMEM_LIMIT),
        name="middle",
    )(summed, inverse, features, upstream, w_self, w_neigh, bias)


def final_kernel(co_ref, first_ref, back_ref, last_ref, base_ref, w_ref, grad_ref, self_ref, neigh_ref, bias_ref):
    carried = total(first_ref[...], back_ref[...], last_ref[...])
    grad_ref[...] = (base_ref[...] + carried).astype(grad_ref.dtype)
    co = co_ref[0]
    self_ref[...] = w_ref[co, :TILE]
    neigh_ref[...] = w_ref[1 - co, :TILE]
    bias_ref[...] = jnp.sum(w_ref[0, TILE:], axis=0, keepdims=True)


def final(co, first, back, last, base, weights):
    shapes = ((base.shape, jnp.bfloat16), ((TILE, TILE), jnp.float32), ((TILE, TILE), jnp.float32), ((1, TILE), jnp.float32))
    args = (first, back, last, base, weights)
    return pl.pallas_call(
        final_kernel,
        grid_spec=pltpu.PrefetchScalarGridSpec(
            num_scalar_prefetch=1,
            grid=(1,),
            in_specs=[whole(x.shape) for x in args],
            out_specs=[whole(x) for x, _ in shapes],
        ),
        out_shape=[jax.ShapeDtypeStruct(x, dtype) for x, dtype in shapes],
        compiler_params=pltpu.CompilerParams(vmem_limit_bytes=VMEM_LIMIT),
        name="final",
    )(co, *args)


STEPS = ((("co", 1),), (("xh", 1),), (), (("z", 4),), (), (("xl", 1),), (("y", 1, 2, 3),), (("z", 1, 2, 3),))


def body(features, tiles, tile_src, tile_dst, tile_count, degree, w_self, w_neigh, bias, upstream):
    held = tiles[0, 0]
    count = tile_count[0]
    co, xl, xh, y = (lax.axis_index(a) for a in ("co", "xl", "xh", "y"))
    live = jnp.arange(held.shape[0], dtype=jnp.int32) < count[0]
    src, dst = tile_src[0, 0], tile_dst[0, 0]
    src = ((((src // 2) % 4) ^ y) * 2 + ((src // 8) ^ xh)) * 2 + src % 2
    src = jnp.where(live, src, 16)
    other = ((dst // 2) % 2) ^ co
    slot = other * 32 + (dst // 4) * 2 + dst % 2
    slot = jnp.where(live, slot, 64)
    inverse = jnp.broadcast_to(1.0 / degree.astype(jnp.float32)[:, None], features.shape)

    blocks = features.reshape(-1, TILE, TILE)
    parts = aggregate(blocks, prepare(features), held, src, slot, count, True, lambda k, *xs: xs)
    hidden, scaled, copies, base, local = middle(
        total(*parts), inverse, features, upstream, w_self, w_neigh, bias.reshape(1, -1)
    )

    weights = [local]

    def side(k, *xs):
        with jax.named_scope("weights"):
            w = weights[0]
            if k == 0:
                mine = lax.dynamic_index_in_dim(w, co, 0, keepdims=False)
                w = mine + flip(lax.dynamic_index_in_dim(w, 1 - co, 0, keepdims=False), "co")
            else:
                for axis, *hops in STEPS[k]:
                    w = sum((flip(w, axis, d) for d in hops), w)
            *xs, weights[0] = tie(*xs, w)
        return xs

    parts = aggregate(scaled.reshape(-1, TILE, TILE), copies, held, src, slot, count, False, side)
    with jax.named_scope("weights"):
        pair = jnp.stack([weights[0], flip(weights[0], "co")])
    grad_features, grad_self, grad_neigh, grad_bias = final(co.reshape(1), *parts, base, pair)
    return hidden, grad_features, grad_self, grad_neigh, grad_bias[0]


def solution(mesh):
    fine = Mesh(mesh.devices.reshape(8, 2, 2, 2, 4), ROW + COL)
    nodes = P(ROW + COL, None)
    return jax.shard_map(
        body,
        mesh=fine,
        in_specs=(
            nodes,
            P(ROW, COL, None, None, None),
            P(ROW, COL, None),
            P(ROW, COL, None),
            P(ROW, COL),
            P(ROW + COL),
            P(),
            P(),
            P(),
            nodes,
        ),
        out_specs=(nodes, nodes, P(), P(), P()),
        check_vma=False,
    )
```

```python
import jax
import jax.numpy as jnp
from jax import lax
from jax.experimental import pallas as pl
from jax.experimental.pallas import tpu as pltpu
from jax.sharding import Mesh
from jax.sharding import PartitionSpec as P

TILE = 128
UNROLL = 8
GROUP = 16
ROW = ("z", "xl", "co")
COL = ("xh", "y")
HALF_SCALE = 2.0
VMEM_LIMIT = 16 * 1024 * 1024


def whole(shape):
    return pl.BlockSpec(shape, lambda *_: (0,) * len(shape))


def multiply(tiles_hbm, tiles_ref, sems, count_ref, acc_ref, ids_ref, prepare, product):
    count = count_ref[0]
    groups = tiles_ref.shape[0] // GROUP

    def chunk(i):
        part = pl.ds(i * GROUP, GROUP)
        return pltpu.make_async_copy(tiles_hbm.at[part], tiles_ref.at[part], sems.at[i])

    for i in range(groups):
        chunk(i).start()
    prepare()
    acc_ref[...] = jnp.zeros_like(acc_ref)

    def step(k, carry):
        base = k * UNROLL
        outs = [product(base + u) for u in range(UNROLL)]
        for u in range(UNROLL):
            acc_ref[ids_ref[base + u]] += outs[u]
        return carry

    last = (count + UNROLL - 1) // UNROLL
    per = GROUP // UNROLL
    for i in range(groups):
        chunk(i).wait()
        lax.fori_loop(jnp.minimum(i * per, last), jnp.minimum((i + 1) * per, last), step, 0)


def ahead_kernel(src_ref, slot_ref, count_ref, f0, f1, f2, f3, tiles_hbm,
                 keep_ref, send_ref, field_ref, acc_ref, tiles_ref, sems):
    def prepare():
        for k, f in enumerate((f0, f1, f2, f3)):
            for h in range(2):
                field_ref[k * 4 + h * 2 : k * 4 + h * 2 + 2] = f[h]
        field_ref[16] = jnp.zeros_like(field_ref[16])

    def product(t):
        return jnp.dot(tiles_ref[t], field_ref[src_ref[t]], preferred_element_type=jnp.float32)

    multiply(tiles_hbm, tiles_ref, sems, count_ref, acc_ref, slot_ref, prepare, product)
    send_ref[...] = acc_ref[32:64].astype(send_ref.dtype)
    keep_ref[...] = acc_ref[:32]


def behind_kernel(src_ref, slot_ref, count_ref, g0, g1, g2, g3, tiles_hbm,
                  keep_ref, s1, s2, s3, field_ref, acc_ref, tiles_ref, sems):
    n = g0.shape[0]

    def prepare():
        for k, g in enumerate((g0, g1, g2, g3)):
            field_ref[k * n : (k + 1) * n] = g[...]
        field_ref[4 * n] = jnp.zeros_like(field_ref[4 * n])

    def product(t):
        return jnp.dot(field_ref[slot_ref[t]], tiles_ref[t], preferred_element_type=jnp.float32)

    multiply(tiles_hbm, tiles_ref, sems, count_ref, acc_ref, src_ref, prepare, product)
    for p, ref in enumerate((keep_ref, s1, s2, s3)):
        for k in range(4):
            ref[k] = acc_ref[p * 4 + k].T.astype(ref.dtype)


def products(kernel, parts, tiles, src, slot, count, nfield, nacc, outs, name):
    n = tiles.shape[0]
    return pl.pallas_call(
        kernel,
        in_specs=[pl.BlockSpec(memory_space=pltpu.SMEM)] * 3
        + [pl.BlockSpec(memory_space=pltpu.VMEM)] * len(parts)
        + [pl.BlockSpec(memory_space=pltpu.HBM)],
        out_specs=[pl.BlockSpec(memory_space=pltpu.VMEM) for _ in outs],
        out_shape=[jax.ShapeDtypeStruct((k, TILE, TILE), dtype) for k, dtype in outs],
        scratch_shapes=[
            pltpu.VMEM((nfield + 1, TILE, TILE), jnp.bfloat16),
            pltpu.VMEM((nacc + 1, TILE, TILE), jnp.float32),
            pltpu.VMEM((n, TILE, TILE), tiles.dtype),
            pltpu.SemaphoreType.DMA((n // GROUP,)),
        ],
        compiler_params=pltpu.CompilerParams(vmem_limit_bytes=VMEM_LIMIT),
        cost_estimate=pl.CostEstimate(
            flops=(16 if name == "ahead" else 2) * n * TILE**3, bytes_accessed=n * TILE * TILE * 2, transcendentals=0
        ),
        name=name,
    )(src, slot, count, *parts, pltpu.with_memory_space_constraint(tiles, pltpu.HBM))


def flip(x, axis, d=1):
    n = lax.axis_size(axis)
    return lax.ppermute(x, axis, [(i, i ^ d) for i in range(n)])


def tie(*xs):
    return lax.optimization_barrier(xs)


def pack(x, exact):
    return (x.astype(jnp.float32) * HALF_SCALE).astype(jnp.float16) if exact else x.astype(jnp.bfloat16)


def unpack(x):
    wide = x.astype(jnp.float32)
    return wide * (1.0 / HALF_SCALE) if x.dtype == jnp.float16 else wide


def aggregate(field, copies, tiles, src, into, out_of, count, exact, side):
    sent = jnp.float32 if exact else jnp.bfloat16
    with jax.named_scope("gather_row"):
        g00 = lax.all_to_all(copies, "z", 0, 0, tiled=True).reshape(-1, TILE, TILE)
    with jax.named_scope("gather_col"):
        (other,) = side(0, flip(field, "xh"))
        pair = jnp.stack([field, other])
        cols = side(1, pair, *(flip(pair, "y", k) for k in (1, 2, 3)))
    g00, *cols = tie(g00, *cols)
    with jax.named_scope("gather_row"):
        g01 = flip(g00, "xl")
        g10 = flip(g00, "co")
    with jax.named_scope("ahead"):
        keep, send = products(
            ahead_kernel, cols, tiles, src, into, count, 16, 64, ((32, jnp.float32), (32, sent)), "ahead"
        )
        keep, send = side(2, keep, send)
    with jax.named_scope("scatter_row"):
        both = pack(keep + unpack(flip(pack(send, exact), "co")), exact)
        (both,) = side(3, both)
        first = lax.all_to_all(both.reshape(16, -1, TILE), ("z", "xl"), 0, 0, tiled=True)
    g01, _ = tie(g01, both)
    with jax.named_scope("gather_row"):
        (g11,) = side(4, flip(g01, "co"))
    with jax.named_scope("behind"):
        back, *sends = products(
            behind_kernel, (g00, g01, g10, g11), tiles, src, out_of, count, 64, 16, ((4, jnp.float32),) + ((4, jnp.bfloat16),) * 3, "behind"
        )
        back, *sends = side(5, back, *sends)
    with jax.named_scope("scatter_col"):
        for k in (1, 2, 3):
            back = back + unpack(flip(sends[k - 1], "y", k))
        (back,) = side(6, back)
        last = flip(pack(back[2:], exact), "xh")
    (last,) = side(7, last)
    return first, back[:2].reshape(-1, TILE), last.reshape(-1, TILE)


def total(first, back, last):
    return jnp.sum(unpack(first), axis=0) + back + unpack(last)


def prepare_kernel(features_ref, copies_ref):
    for h in range(2):
        block = features_ref[h * TILE : (h + 1) * TILE].astype(jnp.float32).T.astype(jnp.bfloat16)
        for k in range(copies_ref.shape[0]):
            copies_ref[k, h] = block


def prepare(features):
    return pl.pallas_call(
        prepare_kernel,
        out_shape=jax.ShapeDtypeStruct((8, 2, TILE, TILE), jnp.bfloat16),
        compiler_params=pltpu.CompilerParams(vmem_limit_bytes=VMEM_LIMIT),
        name="prepare",
    )(features)


def middle_kernel(summed_ref, inverse_ref, features_ref, upstream_ref, w_self_ref, w_neigh_ref, bias_ref,
                  hidden_ref, scaled_ref, copies_ref, base_ref, local_ref):
    def dot(a, b, dims):
        return lax.dot_general(a, b, (dims, ((), ())), preferred_element_type=jnp.float32)

    features = features_ref[...]
    inverse = inverse_ref[...]
    w_self, w_neigh = w_self_ref[...], w_neigh_ref[...]
    agg = (summed_ref[...] * inverse).astype(jnp.bfloat16)
    pre = dot(features, w_self, ((1,), (0,))) + dot(agg, w_neigh, ((1,), (0,))) + bias_ref[...]
    hidden_ref[...] = jnp.maximum(pre, 0.0).astype(jnp.bfloat16)
    wide = jnp.where(pre > 0, upstream_ref[...].astype(jnp.float32), 0.0)
    dpre = wide.astype(jnp.bfloat16)
    scaled = (dot(dpre, w_neigh, ((1,), (1,))) * inverse).astype(jnp.bfloat16)
    scaled_ref[...] = scaled
    for h in range(2):
        block = scaled[h * TILE : (h + 1) * TILE].astype(jnp.float32).T.astype(jnp.bfloat16)
        for k in range(copies_ref.shape[0]):
            copies_ref[k, h] = block
    base_ref[...] = dot(dpre, w_self, ((1,), (1,)))
    local_ref[0, :TILE] = dot(features, dpre, ((0,), (0,)))
    local_ref[1, :TILE] = dot(agg, dpre, ((0,), (0,)))
    wide = wide.reshape(-1, 8, TILE)
    for h in range(2):
        local_ref[h, TILE:] = jnp.sum(wide, axis=0)


def middle(summed, inverse, features, upstream, w_self, w_neigh, bias):
    nodes = features.shape
    return pl.pallas_call(
        middle_kernel,
        out_shape=[
            jax.ShapeDtypeStruct(nodes, jnp.bfloat16),
            jax.ShapeDtypeStruct(nodes, jnp.bfloat16),
            jax.ShapeDtypeStruct((8, 2, TILE, TILE), jnp.bfloat16),
            jax.ShapeDtypeStruct(nodes, jnp.float32),
            jax.ShapeDtypeStruct((2, TILE + 8, TILE), jnp.float32),
        ],
        compiler_params=pltpu.CompilerParams(vmem_limit_bytes=VMEM_LIMIT),
        name="middle",
    )(summed, inverse, features, upstream, w_self, w_neigh, bias)


def final_kernel(co_ref, first_ref, back_ref, last_ref, base_ref, w_ref, grad_ref, self_ref, neigh_ref, bias_ref):
    carried = total(first_ref[...], back_ref[...], last_ref[...])
    grad_ref[...] = (base_ref[...] + carried).astype(grad_ref.dtype)
    co = co_ref[0]
    self_ref[...] = w_ref[co, :TILE]
    neigh_ref[...] = w_ref[1 - co, :TILE]
    bias_ref[...] = jnp.sum(w_ref[0, TILE:], axis=0, keepdims=True)


def final(co, first, back, last, base, weights):
    shapes = ((base.shape, jnp.bfloat16), ((TILE, TILE), jnp.float32), ((TILE, TILE), jnp.float32), ((1, TILE), jnp.float32))
    args = (first, back, last, base, weights)
    return pl.pallas_call(
        final_kernel,
        grid_spec=pltpu.PrefetchScalarGridSpec(
            num_scalar_prefetch=1,
            grid=(1,),
            in_specs=[whole(x.shape) for x in args],
            out_specs=[whole(x) for x, _ in shapes],
        ),
        out_shape=[jax.ShapeDtypeStruct(x, dtype) for x, dtype in shapes],
        compiler_params=pltpu.CompilerParams(vmem_limit_bytes=VMEM_LIMIT),
        name="final",
    )(co, *args)


STEPS = ((("co", 1),), (("xh", 1),), (), (("z", 1),), (), (("xl", 1),), (("y", 1, 2, 3),), (("z", 2, 4, 6),))


def body(features, tiles, tile_src, tile_dst, tile_count, degree, w_self, w_neigh, bias, upstream):
    held = tiles[0, 0]
    count = tile_count[0]
    co, xl, xh, y = (lax.axis_index(a) for a in ("co", "xl", "xh", "y"))
    live = jnp.arange(held.shape[0], dtype=jnp.int32) < count[0]
    src, dst = tile_src[0, 0], tile_dst[0, 0]
    src = ((((src // 2) % 4) ^ y) * 2 + ((src // 8) ^ xh)) * 2 + src % 2
    src = jnp.where(live, src, 16)
    other = ((dst // 2) % 2) ^ co
    into = other * 32 + (dst // 4) * 2 + dst % 2
    into = jnp.where(live, into, 64)
    out_of = (other * 2 + (((dst // 4) % 2) ^ xl)) * 16 + (dst // 8) * 2 + dst % 2
    out_of = jnp.where(live, out_of, 64)
    inverse = jnp.broadcast_to(1.0 / degree.astype(jnp.float32)[:, None], features.shape)

    blocks = features.reshape(-1, TILE, TILE)
    parts = aggregate(blocks, prepare(features), held, src, into, out_of, count, True, lambda k, *xs: xs)
    hidden, scaled, copies, base, local = middle(
        total(*parts), inverse, features, upstream, w_self, w_neigh, bias.reshape(1, -1)
    )

    weights = [local]

    def side(k, *xs):
        with jax.named_scope("weights"):
            w = weights[0]
            if k == 0:
                mine = lax.dynamic_index_in_dim(w, co, 0, keepdims=False)
                w = mine + flip(lax.dynamic_index_in_dim(w, 1 - co, 0, keepdims=False), "co")
            else:
                for axis, *hops in STEPS[k]:
                    w = sum((flip(w, axis, d) for d in hops), w)
            *xs, weights[0] = tie(*xs, w)
        return xs

    parts = aggregate(scaled.reshape(-1, TILE, TILE), copies, held, src, into, out_of, count, False, side)
    with jax.named_scope("weights"):
        pair = jnp.stack([weights[0], flip(weights[0], "co")])
    grad_features, grad_self, grad_neigh, grad_bias = final(co.reshape(1), *parts, base, pair)
    return hidden, grad_features, grad_self, grad_neigh, grad_bias[0]


def solution(mesh):
    fine = Mesh(mesh.devices.reshape(8, 2, 2, 2, 4), ROW + COL)
    nodes = P(ROW + COL, None)
    return jax.shard_map(
        body,
        mesh=fine,
        in_specs=(
            nodes,
            P(ROW, COL, None, None, None),
            P(ROW, COL, None),
            P(ROW, COL, None),
            P(ROW, COL),
            P(ROW + COL),
            P(),
            P(),
            P(),
            nodes,
        ),
        out_specs=(nodes, nodes, P(), P(), P()),
        check_vma=False,
    )
```

```python
import jax
import jax.numpy as jnp
from jax import lax
from jax.experimental import pallas as pl
from jax.experimental.pallas import tpu as pltpu
from jax.sharding import Mesh
from jax.sharding import PartitionSpec as P

TILE = 128
UNROLL = 8
GROUP = 16
ROW = ("z", "xl", "co")
COL = ("xh", "y")
HALF_SCALE = 2.0
VMEM_LIMIT = 16 * 1024 * 1024


def whole(shape):
    return pl.BlockSpec(shape, lambda *_: (0,) * len(shape))


def multiply(tiles_hbm, tiles_ref, sems, count_ref, acc_ref, ids_ref, prepare, product):
    count = count_ref[0]
    groups = tiles_ref.shape[0] // GROUP

    def chunk(i):
        part = pl.ds(i * GROUP, GROUP)
        return pltpu.make_async_copy(tiles_hbm.at[part], tiles_ref.at[part], sems.at[i])

    for i in range(groups):
        chunk(i).start()
    prepare()
    acc_ref[...] = jnp.zeros_like(acc_ref)

    def step(k, carry):
        base = k * UNROLL
        outs = [product(base + u) for u in range(UNROLL)]
        for u in range(UNROLL):
            acc_ref[ids_ref[base + u]] += outs[u]
        return carry

    last = (count + UNROLL - 1) // UNROLL
    per = GROUP // UNROLL
    for i in range(groups):
        chunk(i).wait()
        lax.fori_loop(jnp.minimum(i * per, last), jnp.minimum((i + 1) * per, last), step, 0)


def ahead_kernel(src_ref, slot_ref, count_ref, f0, f1, f2, f3, tiles_hbm,
                 keep_ref, send_ref, field_ref, acc_ref, tiles_ref, sems):
    def prepare():
        for k, f in enumerate((f0, f1, f2, f3)):
            for h in range(2):
                field_ref[k * 4 + h * 2 : k * 4 + h * 2 + 2] = f[h]
        field_ref[16] = jnp.zeros_like(field_ref[16])

    def product(t):
        return jnp.dot(tiles_ref[t], field_ref[src_ref[t]], preferred_element_type=jnp.float32)

    multiply(tiles_hbm, tiles_ref, sems, count_ref, acc_ref, slot_ref, prepare, product)
    send_ref[...] = acc_ref[32:64].astype(send_ref.dtype)
    keep_ref[...] = acc_ref[:32]


def behind_kernel(src_ref, slot_ref, count_ref, g0, g1, tiles_hbm,
                  keep_ref, s1, s2, s3, field_ref, acc_ref, tiles_ref, sems):
    n = g0.shape[0]

    def prepare():
        field_ref[:n] = g0[...]
        field_ref[n : 2 * n] = g1[...]
        field_ref[2 * n] = jnp.zeros_like(field_ref[2 * n])

    def product(t):
        return jnp.dot(field_ref[slot_ref[t]], tiles_ref[t], preferred_element_type=jnp.float32)

    multiply(tiles_hbm, tiles_ref, sems, count_ref, acc_ref, src_ref, prepare, product)
    for p, ref in enumerate((keep_ref, s1, s2, s3)):
        for k in range(4):
            ref[k] = acc_ref[p * 4 + k].T.astype(ref.dtype)


def products(kernel, parts, tiles, src, slot, count, nfield, nacc, outs, name):
    n = tiles.shape[0]
    return pl.pallas_call(
        kernel,
        in_specs=[pl.BlockSpec(memory_space=pltpu.SMEM)] * 3
        + [pl.BlockSpec(memory_space=pltpu.VMEM)] * len(parts)
        + [pl.BlockSpec(memory_space=pltpu.HBM)],
        out_specs=[pl.BlockSpec(memory_space=pltpu.VMEM) for _ in outs],
        out_shape=[jax.ShapeDtypeStruct((k, TILE, TILE), dtype) for k, dtype in outs],
        scratch_shapes=[
            pltpu.VMEM((nfield + 1, TILE, TILE), jnp.bfloat16),
            pltpu.VMEM((nacc + 1, TILE, TILE), jnp.float32),
            pltpu.VMEM((n, TILE, TILE), tiles.dtype),
            pltpu.SemaphoreType.DMA((n // GROUP,)),
        ],
        compiler_params=pltpu.CompilerParams(vmem_limit_bytes=VMEM_LIMIT),
        cost_estimate=pl.CostEstimate(
            flops=16 * n * TILE**3, bytes_accessed=n * TILE * TILE * 2, transcendentals=0
        ),
        name=name,
    )(src, slot, count, *parts, pltpu.with_memory_space_constraint(tiles, pltpu.HBM))


def flip(x, axis, d=1):
    n = lax.axis_size(axis)
    return lax.ppermute(x, axis, [(i, i ^ d) for i in range(n)])


def tie(*xs):
    return lax.optimization_barrier(xs)


def pack(x, exact):
    return (x.astype(jnp.float32) * HALF_SCALE).astype(jnp.float16) if exact else x.astype(jnp.bfloat16)


def unpack(x):
    wide = x.astype(jnp.float32)
    return wide * (1.0 / HALF_SCALE) if x.dtype == jnp.float16 else wide


def aggregate(field, copies, tiles, src, slot, count, exact, side):
    sent = jnp.float32 if exact else jnp.bfloat16
    with jax.named_scope("gather_row"):
        g0 = lax.all_to_all(copies, ("z", "xl"), 0, 0, tiled=True).reshape(-1, TILE, TILE)
    with jax.named_scope("gather_col"):
        (other,) = side(0, flip(field, "xh"))
        pair = jnp.stack([field, other])
        cols = side(1, pair, *(flip(pair, "y", k) for k in (1, 2, 3)))
    with jax.named_scope("ahead"):
        keep, send = products(
            ahead_kernel, cols, tiles, src, slot, count, 16, 64, ((32, jnp.float32), (32, sent)), "ahead"
        )
        keep, send = side(2, keep, send)
    with jax.named_scope("scatter_row"):
        both = pack(keep + unpack(flip(pack(send, exact), "co")), exact)
    g0, both = tie(*side(3, g0), both)
    with jax.named_scope("scatter_row"):
        first = lax.all_to_all(both.reshape(16, -1, TILE), ("z", "xl"), 0, 0, tiled=True)
    with jax.named_scope("gather_row"):
        (g1,) = side(4, flip(g0, "co"))
    with jax.named_scope("behind"):
        back, *sends = products(
            behind_kernel, (g0, g1), tiles, src, slot, count, 64, 16, ((4, jnp.float32),) + ((4, sent),) * 3, "behind"
        )
        back, *sends = side(5, back, *sends)
    with jax.named_scope("scatter_col"):
        for k in (1, 2, 3):
            back = back + unpack(flip(pack(sends[k - 1], exact), "y", k))
        (back,) = side(6, back)
        last = flip(pack(back[2:], exact), "xh")
    (last,) = side(7, last)
    return first, back[:2].reshape(-1, TILE), last.reshape(-1, TILE)


def total(first, back, last):
    return jnp.sum(unpack(first), axis=0) + back + unpack(last)


def prepare_kernel(features_ref, copies_ref):
    for h in range(2):
        block = features_ref[h * TILE : (h + 1) * TILE].astype(jnp.float32).T.astype(jnp.bfloat16)
        for k in range(copies_ref.shape[0]):
            copies_ref[k, h] = block


def prepare(features):
    return pl.pallas_call(
        prepare_kernel,
        out_shape=jax.ShapeDtypeStruct((16, 2, TILE, TILE), jnp.bfloat16),
        compiler_params=pltpu.CompilerParams(vmem_limit_bytes=VMEM_LIMIT),
        name="prepare",
    )(features)


def middle_kernel(summed_ref, inverse_ref, features_ref, upstream_ref, w_self_ref, w_neigh_ref, bias_ref,
                  hidden_ref, scaled_ref, copies_ref, base_ref, local_ref):
    def dot(a, b, dims):
        return lax.dot_general(a, b, (dims, ((), ())), preferred_element_type=jnp.float32)

    features = features_ref[...]
    inverse = inverse_ref[...]
    w_self, w_neigh = w_self_ref[...], w_neigh_ref[...]
    agg = (summed_ref[...] * inverse).astype(jnp.bfloat16)
    pre = dot(features, w_self, ((1,), (0,))) + dot(agg, w_neigh, ((1,), (0,))) + bias_ref[...]
    hidden_ref[...] = jnp.maximum(pre, 0.0).astype(jnp.bfloat16)
    wide = jnp.where(pre > 0, upstream_ref[...].astype(jnp.float32), 0.0)
    dpre = wide.astype(jnp.bfloat16)
    scaled = (dot(dpre, w_neigh, ((1,), (1,))) * inverse).astype(jnp.bfloat16)
    scaled_ref[...] = scaled
    for h in range(2):
        block = scaled[h * TILE : (h + 1) * TILE].astype(jnp.float32).T.astype(jnp.bfloat16)
        for k in range(copies_ref.shape[0]):
            copies_ref[k, h] = block
    base_ref[...] = dot(dpre, w_self, ((1,), (1,)))
    local_ref[0, :TILE] = dot(features, dpre, ((0,), (0,)))
    local_ref[1, :TILE] = dot(agg, dpre, ((0,), (0,)))
    wide = wide.reshape(-1, 8, TILE)
    for h in range(2):
        local_ref[h, TILE:] = jnp.sum(wide, axis=0)


def middle(summed, inverse, features, upstream, w_self, w_neigh, bias):
    nodes = features.shape
    return pl.pallas_call(
        middle_kernel,
        out_shape=[
            jax.ShapeDtypeStruct(nodes, jnp.bfloat16),
            jax.ShapeDtypeStruct(nodes, jnp.bfloat16),
            jax.ShapeDtypeStruct((16, 2, TILE, TILE), jnp.bfloat16),
            jax.ShapeDtypeStruct(nodes, jnp.float32),
            jax.ShapeDtypeStruct((2, TILE + 8, TILE), jnp.float32),
        ],
        compiler_params=pltpu.CompilerParams(vmem_limit_bytes=VMEM_LIMIT),
        name="middle",
    )(summed, inverse, features, upstream, w_self, w_neigh, bias)


def final_kernel(co_ref, first_ref, back_ref, last_ref, base_ref, w_ref, grad_ref, self_ref, neigh_ref, bias_ref):
    carried = total(first_ref[...], back_ref[...], last_ref[...])
    grad_ref[...] = (base_ref[...] + carried).astype(grad_ref.dtype)
    co = co_ref[0]
    self_ref[...] = w_ref[co, :TILE]
    neigh_ref[...] = w_ref[1 - co, :TILE]
    bias_ref[...] = jnp.sum(w_ref[0, TILE:], axis=0, keepdims=True)


def final(co, first, back, last, base, weights):
    shapes = ((base.shape, jnp.bfloat16), ((TILE, TILE), jnp.float32), ((TILE, TILE), jnp.float32), ((1, TILE), jnp.float32))
    args = (first, back, last, base, weights)
    return pl.pallas_call(
        final_kernel,
        grid_spec=pltpu.PrefetchScalarGridSpec(
            num_scalar_prefetch=1,
            grid=(1,),
            in_specs=[whole(x.shape) for x in args],
            out_specs=[whole(x) for x, _ in shapes],
        ),
        out_shape=[jax.ShapeDtypeStruct(x, dtype) for x, dtype in shapes],
        compiler_params=pltpu.CompilerParams(vmem_limit_bytes=VMEM_LIMIT),
        name="final",
    )(co, *args)


STEPS = ((("co", 1),), (("xh", 1),), (), (("z", 6),), (), (("xl", 1),), (("y", 1, 2, 3),), (("z", 1, 2, 3),))


def body(features, tiles, tile_src, tile_dst, tile_count, degree, w_self, w_neigh, bias, upstream):
    held = tiles[0, 0]
    count = tile_count[0]
    co, xl, xh, y = (lax.axis_index(a) for a in ("co", "xl", "xh", "y"))
    live = jnp.arange(held.shape[0], dtype=jnp.int32) < count[0]
    src, dst = tile_src[0, 0], tile_dst[0, 0]
    src = ((((src // 2) % 4) ^ y) * 2 + ((src // 8) ^ xh)) * 2 + src % 2
    src = jnp.where(live, src, 16)
    other = ((dst // 2) % 2) ^ co
    slot = other * 32 + (dst // 4) * 2 + dst % 2
    slot = jnp.where(live, slot, 64)
    inverse = jnp.broadcast_to(1.0 / degree.astype(jnp.float32)[:, None], features.shape)

    blocks = features.reshape(-1, TILE, TILE)
    parts = aggregate(blocks, prepare(features), held, src, slot, count, True, lambda k, *xs: xs)
    hidden, scaled, copies, base, local = middle(
        total(*parts), inverse, features, upstream, w_self, w_neigh, bias.reshape(1, -1)
    )

    weights = [local]

    def side(k, *xs):
        with jax.named_scope("weights"):
            w = weights[0]
            if k == 0:
                mine = lax.dynamic_index_in_dim(w, co, 0, keepdims=False)
                w = mine + flip(lax.dynamic_index_in_dim(w, 1 - co, 0, keepdims=False), "co")
            else:
                for axis, *hops in STEPS[k]:
                    w = sum((flip(w, axis, d) for d in hops), w)
            *xs, weights[0] = tie(*xs, w)
        return xs

    parts = aggregate(scaled.reshape(-1, TILE, TILE), copies, held, src, slot, count, False, side)
    with jax.named_scope("weights"):
        pair = jnp.stack([weights[0], flip(weights[0], "co")])
    grad_features, grad_self, grad_neigh, grad_bias = final(co.reshape(1), *parts, base, pair)
    return hidden, grad_features, grad_self, grad_neigh, grad_bias[0]


def solution(mesh):
    fine = Mesh(mesh.devices.reshape(8, 2, 2, 2, 4), ROW + COL)
    nodes = P(ROW + COL, None)
    return jax.shard_map(
        body,
        mesh=fine,
        in_specs=(
            nodes,
            P(ROW, COL, None, None, None),
            P(ROW, COL, None),
            P(ROW, COL, None),
            P(ROW, COL),
            P(ROW + COL),
            P(),
            P(),
            P(),
            nodes,
        ),
        out_specs=(nodes, nodes, P(), P(), P()),
        check_vma=False,
    )
```

```python
import jax
import jax.numpy as jnp
from jax import lax
from jax.experimental import pallas as pl
from jax.experimental.pallas import tpu as pltpu
from jax.sharding import Mesh
from jax.sharding import PartitionSpec as P

TILE = 128
UNROLL = 8
GROUP = 16
ROW = ("z", "xl", "co")
COL = ("xh", "y")
HALF_SCALE = 2.0
VMEM_LIMIT = 16 * 1024 * 1024


def whole(shape):
    return pl.BlockSpec(shape, lambda *_: (0,) * len(shape))


def multiply(tiles_hbm, tiles_ref, sems, count_ref, acc_ref, ids_ref, prepare, product):
    count = count_ref[0]
    groups = tiles_ref.shape[0] // GROUP

    def chunk(i):
        part = pl.ds(i * GROUP, GROUP)
        return pltpu.make_async_copy(tiles_hbm.at[part], tiles_ref.at[part], sems.at[i])

    for i in range(groups):
        chunk(i).start()
    prepare()
    acc_ref[...] = jnp.zeros_like(acc_ref)

    def step(k, carry):
        base = k * UNROLL
        outs = [product(base + u) for u in range(UNROLL)]
        for u in range(UNROLL):
            acc_ref[ids_ref[base + u]] += outs[u]
        return carry

    last = (count + UNROLL - 1) // UNROLL
    per = GROUP // UNROLL
    for i in range(groups):
        chunk(i).wait()
        lax.fori_loop(jnp.minimum(i * per, last), jnp.minimum((i + 1) * per, last), step, 0)


def ahead_kernel(src_ref, slot_ref, count_ref, f0, f1, f2, f3, tiles_hbm,
                 keep_ref, send_ref, field_ref, acc_ref, tiles_ref, sems):
    def prepare():
        for k, f in enumerate((f0, f1, f2, f3)):
            for h in range(2):
                field_ref[k * 4 + h * 2 : k * 4 + h * 2 + 2] = f[h]
        field_ref[16] = jnp.zeros_like(field_ref[16])

    def product(t):
        return jnp.dot(tiles_ref[t], field_ref[src_ref[t]], preferred_element_type=jnp.float32)

    multiply(tiles_hbm, tiles_ref, sems, count_ref, acc_ref, slot_ref, prepare, product)
    send_ref[...] = acc_ref[32:64].astype(send_ref.dtype)
    keep_ref[...] = acc_ref[:32]


def behind_kernel(src_ref, slot_ref, count_ref, g0, g1, g2, g3, tiles_hbm,
                  keep_ref, s1, s2, s3, field_ref, acc_ref, tiles_ref, sems):
    n = g0.shape[0]

    def prepare():
        for k, g in enumerate((g0, g1, g2, g3)):
            field_ref[k * n : (k + 1) * n] = g[...]
        field_ref[4 * n] = jnp.zeros_like(field_ref[4 * n])

    def product(t):
        return jnp.dot(field_ref[slot_ref[t]], tiles_ref[t], preferred_element_type=jnp.float32)

    multiply(tiles_hbm, tiles_ref, sems, count_ref, acc_ref, src_ref, prepare, product)
    for p, ref in enumerate((keep_ref, s1, s2, s3)):
        for k in range(4):
            ref[k] = acc_ref[p * 4 + k].T.astype(ref.dtype)


def products(kernel, parts, tiles, src, slot, count, nfield, nacc, outs, name):
    n = tiles.shape[0]
    return pl.pallas_call(
        kernel,
        in_specs=[pl.BlockSpec(memory_space=pltpu.SMEM)] * 3
        + [pl.BlockSpec(memory_space=pltpu.VMEM)] * len(parts)
        + [pl.BlockSpec(memory_space=pltpu.HBM)],
        out_specs=[pl.BlockSpec(memory_space=pltpu.VMEM) for _ in outs],
        out_shape=[jax.ShapeDtypeStruct((k, TILE, TILE), dtype) for k, dtype in outs],
        scratch_shapes=[
            pltpu.VMEM((nfield + 1, TILE, TILE), jnp.bfloat16),
            pltpu.VMEM((nacc + 1, TILE, TILE), jnp.float32),
            pltpu.VMEM((n, TILE, TILE), tiles.dtype),
            pltpu.SemaphoreType.DMA((n // GROUP,)),
        ],
        compiler_params=pltpu.CompilerParams(vmem_limit_bytes=VMEM_LIMIT),
        cost_estimate=pl.CostEstimate(
            flops=(16 if name == "ahead" else 2) * n * TILE**3, bytes_accessed=n * TILE * TILE * 2, transcendentals=0
        ),
        name=name,
    )(src, slot, count, *parts, pltpu.with_memory_space_constraint(tiles, pltpu.HBM))


def flip(x, axis, d=1):
    n = lax.axis_size(axis)
    return lax.ppermute(x, axis, [(i, i ^ d) for i in range(n)])


def tie(*xs):
    return lax.optimization_barrier(xs)


def pack(x, exact):
    return (x.astype(jnp.float32) * HALF_SCALE).astype(jnp.float16) if exact else x.astype(jnp.bfloat16)


def unpack(x):
    wide = x.astype(jnp.float32)
    return wide * (1.0 / HALF_SCALE) if x.dtype == jnp.float16 else wide


def aggregate(field, copies, tiles, src, into, out_of, count, exact, side):
    sent = jnp.float32 if exact else jnp.bfloat16
    with jax.named_scope("gather_row"):
        g00 = lax.all_to_all(copies, "z", 0, 0, tiled=True).reshape(-1, TILE, TILE)
    with jax.named_scope("gather_col"):
        (other,) = side(0, flip(field, "xh"))
        pair = jnp.stack([field, other])
        cols = side(1, pair, *(flip(pair, "y", k) for k in (1, 2, 3)))
    g00, *cols = tie(g00, *cols)
    with jax.named_scope("gather_row"):
        g01 = flip(g00, "xl")
        g10 = flip(g00, "co")
    with jax.named_scope("ahead"):
        keep, send = products(
            ahead_kernel, cols, tiles, src, into, count, 16, 64, ((32, jnp.float32), (32, sent)), "ahead"
        )
        keep, send = side(2, keep, send)
    with jax.named_scope("scatter_row"):
        both = pack(keep + unpack(flip(pack(send, exact), "co")), exact)
        (both,) = side(3, both)
        first = lax.all_to_all(both.reshape(16, -1, TILE), ("z", "xl"), 0, 0, tiled=True)
    g01, _ = tie(g01, both)
    with jax.named_scope("gather_row"):
        (g11,) = side(4, flip(g01, "co"))
    with jax.named_scope("behind"):
        back, *sends = products(
            behind_kernel, (g00, g01, g10, g11), tiles, src, out_of, count, 64, 16, ((4, jnp.float32),) + ((4, jnp.bfloat16),) * 3, "behind"
        )
        back, *sends = side(5, back, *sends)
    with jax.named_scope("scatter_col"):
        for k in (1, 2, 3):
            back = back + unpack(flip(sends[k - 1], "y", k))
        (back,) = side(6, back)
        last = flip(pack(back[2:], exact), "xh")
    (last,) = side(7, last)
    return first, back[:2].reshape(-1, TILE), last.reshape(-1, TILE)


def total(first, back, last):
    return jnp.sum(unpack(first), axis=0) + back + unpack(last)


def prepare_kernel(features_ref, copies_ref):
    for h in range(2):
        block = features_ref[h * TILE : (h + 1) * TILE].astype(jnp.float32).T.astype(jnp.bfloat16)
        for k in range(copies_ref.shape[0]):
            copies_ref[k, h] = block


def prepare(features):
    return pl.pallas_call(
        prepare_kernel,
        out_shape=jax.ShapeDtypeStruct((8, 2, TILE, TILE), jnp.bfloat16),
        compiler_params=pltpu.CompilerParams(vmem_limit_bytes=VMEM_LIMIT),
        name="prepare",
    )(features)


def middle_kernel(summed_ref, inverse_ref, features_ref, upstream_ref, w_self_ref, w_neigh_ref, bias_ref,
                  hidden_ref, scaled_ref, copies_ref, base_ref, local_ref):
    def dot(a, b, dims):
        return lax.dot_general(a, b, (dims, ((), ())), preferred_element_type=jnp.float32)

    features = features_ref[...]
    inverse = inverse_ref[...]
    w_self, w_neigh = w_self_ref[...], w_neigh_ref[...]
    agg = (summed_ref[...] * inverse).astype(jnp.bfloat16)
    pre = dot(features, w_self, ((1,), (0,))) + dot(agg, w_neigh, ((1,), (0,))) + bias_ref[...]
    hidden_ref[...] = jnp.maximum(pre, 0.0).astype(jnp.bfloat16)
    wide = jnp.where(pre > 0, upstream_ref[...].astype(jnp.float32), 0.0)
    dpre = wide.astype(jnp.bfloat16)
    scaled = (dot(dpre, w_neigh, ((1,), (1,))) * inverse).astype(jnp.bfloat16)
    scaled_ref[...] = scaled
    for h in range(2):
        block = scaled[h * TILE : (h + 1) * TILE].astype(jnp.float32).T.astype(jnp.bfloat16)
        for k in range(copies_ref.shape[0]):
            copies_ref[k, h] = block
    base_ref[...] = dot(dpre, w_self, ((1,), (1,)))
    local_ref[0, :TILE] = dot(features, dpre, ((0,), (0,)))
    local_ref[1, :TILE] = dot(agg, dpre, ((0,), (0,)))
    wide = wide.reshape(-1, 8, TILE)
    for h in range(2):
        local_ref[h, TILE:] = jnp.sum(wide, axis=0)


def middle(summed, inverse, features, upstream, w_self, w_neigh, bias):
    nodes = features.shape
    return pl.pallas_call(
        middle_kernel,
        out_shape=[
            jax.ShapeDtypeStruct(nodes, jnp.bfloat16),
            jax.ShapeDtypeStruct(nodes, jnp.bfloat16),
            jax.ShapeDtypeStruct((8, 2, TILE, TILE), jnp.bfloat16),
            jax.ShapeDtypeStruct(nodes, jnp.float32),
            jax.ShapeDtypeStruct((2, TILE + 8, TILE), jnp.float32),
        ],
        compiler_params=pltpu.CompilerParams(vmem_limit_bytes=VMEM_LIMIT),
        name="middle",
    )(summed, inverse, features, upstream, w_self, w_neigh, bias)


def final_kernel(co_ref, first_ref, back_ref, last_ref, base_ref, w_ref, grad_ref, self_ref, neigh_ref, bias_ref):
    carried = total(first_ref[...], back_ref[...], last_ref[...])
    grad_ref[...] = (base_ref[...] + carried).astype(grad_ref.dtype)
    co = co_ref[0]
    self_ref[...] = w_ref[co, :TILE]
    neigh_ref[...] = w_ref[1 - co, :TILE]
    bias_ref[...] = jnp.sum(w_ref[0, TILE:], axis=0, keepdims=True)


def final(co, first, back, last, base, weights):
    shapes = ((base.shape, jnp.bfloat16), ((TILE, TILE), jnp.float32), ((TILE, TILE), jnp.float32), ((1, TILE), jnp.float32))
    args = (first, back, last, base, weights)
    return pl.pallas_call(
        final_kernel,
        grid_spec=pltpu.PrefetchScalarGridSpec(
            num_scalar_prefetch=1,
            grid=(1,),
            in_specs=[whole(x.shape) for x in args],
            out_specs=[whole(x) for x, _ in shapes],
        ),
        out_shape=[jax.ShapeDtypeStruct(x, dtype) for x, dtype in shapes],
        compiler_params=pltpu.CompilerParams(vmem_limit_bytes=VMEM_LIMIT),
        name="final",
    )(co, *args)


STEPS = ((("co", 1),), (("xh", 1),), (), (("z", 6),), (), (("xl", 1),), (("y", 1, 2, 3),), (("z", 1, 2, 3),))


def body(features, tiles, tile_src, tile_dst, tile_count, degree, w_self, w_neigh, bias, upstream):
    held = tiles[0, 0]
    count = tile_count[0]
    co, xl, xh, y = (lax.axis_index(a) for a in ("co", "xl", "xh", "y"))
    live = jnp.arange(held.shape[0], dtype=jnp.int32) < count[0]
    src, dst = tile_src[0, 0], tile_dst[0, 0]
    src = ((((src // 2) % 4) ^ y) * 2 + ((src // 8) ^ xh)) * 2 + src % 2
    src = jnp.where(live, src, 16)
    other = ((dst // 2) % 2) ^ co
    into = other * 32 + (dst // 4) * 2 + dst % 2
    into = jnp.where(live, into, 64)
    out_of = (other * 2 + (((dst // 4) % 2) ^ xl)) * 16 + (dst // 8) * 2 + dst % 2
    out_of = jnp.where(live, out_of, 64)
    inverse = jnp.broadcast_to(1.0 / degree.astype(jnp.float32)[:, None], features.shape)

    blocks = features.reshape(-1, TILE, TILE)
    parts = aggregate(blocks, prepare(features), held, src, into, out_of, count, True, lambda k, *xs: xs)
    hidden, scaled, copies, base, local = middle(
        total(*parts), inverse, features, upstream, w_self, w_neigh, bias.reshape(1, -1)
    )

    weights = [local]

    def side(k, *xs):
        with jax.named_scope("weights"):
            w = weights[0]
            if k == 0:
                mine = lax.dynamic_index_in_dim(w, co, 0, keepdims=False)
                w = mine + flip(lax.dynamic_index_in_dim(w, 1 - co, 0, keepdims=False), "co")
            else:
                for axis, *hops in STEPS[k]:
                    w = sum((flip(w, axis, d) for d in hops), w)
            *xs, weights[0] = tie(*xs, w)
        return xs

    parts = aggregate(scaled.reshape(-1, TILE, TILE), copies, held, src, into, out_of, count, False, side)
    with jax.named_scope("weights"):
        pair = jnp.stack([weights[0], flip(weights[0], "co")])
    grad_features, grad_self, grad_neigh, grad_bias = final(co.reshape(1), *parts, base, pair)
    return hidden, grad_features, grad_self, grad_neigh, grad_bias[0]


def solution(mesh):
    fine = Mesh(mesh.devices.reshape(8, 2, 2, 2, 4), ROW + COL)
    nodes = P(ROW + COL, None)
    return jax.shard_map(
        body,
        mesh=fine,
        in_specs=(
            nodes,
            P(ROW, COL, None, None, None),
            P(ROW, COL, None),
            P(ROW, COL, None),
            P(ROW, COL),
            P(ROW + COL),
            P(),
            P(),
            P(),
            nodes,
        ),
        out_specs=(nodes, nodes, P(), P(), P()),
        check_vma=False,
    )
```
